32 devices in a mesh: ax: 8 (over y, x, core), rad: 4 (over z).
Axes of the slice: x: 2, y: 2, z: 4, core: 2. Of those that a mesh axis runs over, the one named last changes fastest.
Arguments:
- leaf_maps: float32 [16, 8, 512, 512], P('ax', 'rad'), may hold values from -0.5 to 22, as said below
- leaf_fluxes: float32 [16, 8, 512], P('ax', 'rad'), may hold values from -6 to 6
Outputs:
- merged_maps: float32 [8, 4, 512, 2048], P('ax', 'rad')
- merged_fluxes: float32 [8, 4, 512], P('ax', 'rad')
The draws below stay inside these ranges and needn't reach their ends.
Inputs may be any that keep to these rules, and one draw needn't show every extreme that they name: `leaf_maps`: every leaf map is symmetric and positive definite, with smallest eigenvalue at least 0.5.
All inputs are finite; a program needn't handle non-finite values.
Results may differ from the reference program's by a relative error of at most 0.0003.
Values sent between devices are 32-bit elements; how exact they have to be, the bound alone decides.
A program may use at most 192 MiB of HBM per device.

```python
import math
import jax
import jax.numpy as jnp
from jax import lax

LEAF = 128
LEAVES_AX = 16
LEAVES_RAD = 8
N_AX = 8
N_RAD = 4


def draw_leaf_maps(key, part):
    matrix_order = 4 * LEAF
    noise_key, diagonal_key, scale_key = jax.random.split(key, 3)
    noise = jax.random.uniform(noise_key, (LEAVES_AX, LEAVES_RAD, matrix_order, matrix_order), jnp.float32, -1.0, 1.0)
    noise = noise * (1.5 * math.sqrt(3.0) / math.sqrt(matrix_order))
    symmetric = (noise + jnp.swapaxes(noise, 2, 3)) * (1.0 / math.sqrt(2.0))
    diagonal = jax.random.uniform(diagonal_key, (LEAVES_AX, LEAVES_RAD, matrix_order), jnp.float32, 4.0, 6.0)
    position = jnp.arange(matrix_order, dtype=jnp.int32)
    side = position // LEAF
    offset = (position % LEAF).astype(jnp.float32) + 0.5
    edge_length = jnp.float32(LEAF)
    zero_line = jnp.zeros_like(offset)
    axial_coord = jnp.where(side == 0, zero_line, jnp.where(side == 1, zero_line + edge_length, offset))
    radial_coord = jnp.where(side == 2, zero_line, jnp.where(side == 3, zero_line + edge_length, offset))
    axial_gap = axial_coord[:, None] - axial_coord[None, :]
    radial_gap = radial_coord[:, None] - radial_coord[None, :]
    distance = jnp.sqrt(axial_gap * axial_gap + radial_gap * radial_gap)
    kernel = jnp.exp(-distance * (4.0 / LEAF))
    weights = jnp.exp(jax.random.uniform(scale_key, (LEAVES_AX, LEAVES_RAD, matrix_order), jnp.float32, 0.0, math.log(4.0)))
    root_scale = jnp.sqrt(weights)
    identity = jnp.eye(matrix_order, dtype=jnp.float32)
    coupled = 2.0 * kernel * root_scale[..., :, None] * root_scale[..., None, :]
    return coupled + symmetric * (1.0 - identity) + diagonal[..., None] * identity


def level_of(key, dims, cuts, smallest, largest):
    gain = 1.0
    for axis_at, parts in cuts:
        steps = jax.random.uniform(jax.random.fold_in(jax.random.fold_in(key, 6), axis_at), (parts,), jnp.float32, smallest / len(cuts), largest / len(cuts))
        gain = gain * jnp.repeat(jnp.exp(steps), dims[axis_at] // parts).reshape((-1,) + (1,) * (len(dims) - 1 - axis_at))
    return gain


def normal_values(own_key, dims, spread, bound, cuts=(), kind=jnp.bfloat16):
    values = spread * jax.random.normal(own_key, dims, jnp.float32)
    if cuts:
        values = values * level_of(own_key, dims, cuts, -0.22, 0.18)
    return jnp.clip(values, -bound, bound).astype(kind)


def setup_inputs(seed: int = 0) -> dict:
    key_list = jax.random.split(jax.random.key(seed), 3)
    return {
        "leaf_maps": draw_leaf_maps(jax.random.fold_in(key_list[2], 71), 0),
        "leaf_fluxes": normal_values(key_list[1], (LEAVES_AX, LEAVES_RAD, 4 * LEAF), 1.0, 6.0, ((0, 8), (1, 4)), jnp.float32),
    }


def leaf_points(axial_leaf, radial_leaf, extent):
    points = []
    for offset in range(extent):
        points.append((0, axial_leaf * extent, radial_leaf * extent + offset))
    for offset in range(extent):
        points.append((0, (axial_leaf + 1) * extent, radial_leaf * extent + offset))
    for offset in range(extent):
        points.append((1, radial_leaf * extent, axial_leaf * extent + offset))
    for offset in range(extent):
        points.append((1, (radial_leaf + 1) * extent, axial_leaf * extent + offset))
    return points

def shifted(points, axial_shift, radial_shift):
    result = []
    for facing, line_pos, coordinate in points:
        if facing == 0:
            result.append((0, line_pos + axial_shift, coordinate + radial_shift))
        else:
            result.append((1, line_pos + radial_shift, coordinate + axial_shift))
    return result

def merge_plan(lower_pts, upper_pts):
    upper_place = {}
    for number, location in enumerate(upper_pts):
        upper_place[location] = number
    lower_inner = [number for number, location in enumerate(lower_pts) if location in upper_place]
    upper_inner = [upper_place[lower_pts[number]] for number in lower_inner]
    lower_outer = [number for number, location in enumerate(lower_pts) if location not in upper_place]
    inner_set = set(upper_inner)
    upper_outer = [number for number in range(len(upper_pts)) if number not in inner_set]
    merged = [lower_pts[number] for number in lower_outer] + [upper_pts[number] for number in upper_outer]
    return ((lower_inner, upper_inner, lower_outer, upper_outer), merged)

def layouts(extent):
    plan_low, pair_low = merge_plan(leaf_points(0, 0, extent), leaf_points(1, 0, extent))
    plan_high, pair_high = merge_plan(leaf_points(0, 1, extent), leaf_points(1, 1, extent))
    plan_block, block_pts = merge_plan(pair_low, pair_high)
    plan_first, first_pts = merge_plan(block_pts, shifted(block_pts, 0, 2 * extent))
    plan_second, second_pts = merge_plan(first_pts, shifted(first_pts, 2 * extent, 0))
    return (plan_low, plan_high, plan_block, plan_first, plan_second)

def find_runs(indices):
    spans = []
    opening = indices[0]
    extent = 1
    for former, latter in zip(indices[:-1], indices[1:]):
        if latter == former + 1:
            extent += 1
        else:
            spans.append((opening, extent))
            opening = latter
            extent = 1
    spans.append((opening, extent))
    return spans

def select_runs(values, indices, dimension):
    pieces = [lax.slice_in_dim(values, opening, opening + extent, axis=dimension) for opening, extent in find_runs(indices)]
    if len(pieces) == 1:
        return pieces[0]
    return jnp.concatenate(pieces, axis=dimension)

def block_of(matrix, row_list, column_list):
    return select_runs(select_runs(matrix, row_list, 0), column_list, 1)

def eliminate(schur_block, coupling, hint):
    factor = jnp.linalg.cholesky(schur_block)
    scaled_rows = lax.linalg.triangular_solve(factor, coupling, left_side=False, lower=True, transpose_a=True)
    solved = lax.linalg.triangular_solve(factor, hint[:, None], left_side=True, lower=True)[:, 0]
    return (scaled_rows, solved)

def dense_merge(lower_map, lower_flux, upper_map, upper_flux, plan):
    lower_inner, upper_inner, lower_outer, upper_outer = plan
    schur_block = block_of(lower_map, lower_inner, lower_inner) + block_of(upper_map, upper_inner, upper_inner)
    coupling = jnp.concatenate([block_of(lower_map, lower_outer, lower_inner), block_of(upper_map, upper_outer, upper_inner)], axis=0)
    hint = select_runs(lower_flux, lower_inner, 0) + select_runs(upper_flux, upper_inner, 0)
    scaled_rows, solved = eliminate(schur_block, coupling, hint)
    lower_square = block_of(lower_map, lower_outer, lower_outer)
    upper_square = block_of(upper_map, upper_outer, upper_outer)
    top_rows = jnp.concatenate([lower_square, jnp.zeros((lower_square.shape[0], upper_square.shape[1]), jnp.float32)], axis=1)
    bottom_rows = jnp.concatenate([jnp.zeros((upper_square.shape[0], lower_square.shape[1]), jnp.float32), upper_square], axis=1)
    diagonal = jnp.concatenate([top_rows, bottom_rows], axis=0)
    outer_flux = jnp.concatenate([select_runs(lower_flux, lower_outer, 0), select_runs(upper_flux, upper_outer, 0)], axis=0)
    merged_map = diagonal - jnp.dot(scaled_rows, scaled_rows.T, precision=lax.Precision.HIGHEST)
    merged_flux = outer_flux - jnp.dot(scaled_rows, solved, precision=lax.Precision.HIGHEST)
    return (merged_map, merged_flux)

def reference(leaf_maps, leaf_fluxes):
    extent = LEAF
    plan_low, plan_high, plan_block, plan_first, plan_second = layouts(extent)
    half_ax = N_AX // 2
    half_rad = N_RAD // 2
    group_count = half_ax * half_rad

    def one_group(number):
        group_ax = (number // half_rad).astype(jnp.int32)
        group_rad = (number % half_rad).astype(jnp.int32)
        nought = jnp.zeros((), jnp.int32)

        def device_box(axial_half, radial_half):
            axial_start = (2 * (group_ax + axial_half * half_ax)).astype(jnp.int32)
            radial_start = (2 * (group_rad + radial_half * half_rad)).astype(jnp.int32)
            maps = lax.dynamic_slice(leaf_maps, (axial_start, radial_start, nought, nought), (2, 2, 4 * extent, 4 * extent))
            fluxes = lax.dynamic_slice(leaf_fluxes, (axial_start, radial_start, nought), (2, 2, 4 * extent))
            lower_pair = dense_merge(maps[0, 0], fluxes[0, 0], maps[1, 0], fluxes[1, 0], plan_low)
            upper_pair = dense_merge(maps[0, 1], fluxes[0, 1], maps[1, 1], fluxes[1, 1], plan_high)
            return dense_merge(lower_pair[0], lower_pair[1], upper_pair[0], upper_pair[1], plan_block)
        pair_results = []
        for axial_half in range(2):
            lower_box = device_box(axial_half, 0)
            upper_box = device_box(axial_half, 1)
            pair_results.append(dense_merge(lower_box[0], lower_box[1], upper_box[0], upper_box[1], plan_first))
        final_map, final_flux = dense_merge(pair_results[0][0], pair_results[0][1], pair_results[1][0], pair_results[1][1], plan_second)
        return (final_map.reshape(2, 2, 4 * extent, 16 * extent), final_flux.reshape(2, 2, 4 * extent))
    all_maps, all_fluxes = lax.map(one_group, jnp.arange(group_count, dtype=jnp.int32))
    all_maps = all_maps.reshape(half_ax, half_rad, 2, 2, 4 * extent, 16 * extent)
    all_maps = all_maps.transpose(2, 0, 3, 1, 4, 5).reshape(N_AX, N_RAD, 4 * extent, 16 * extent)
    all_fluxes = all_fluxes.reshape(half_ax, half_rad, 2, 2, 4 * extent)
    all_fluxes = all_fluxes.transpose(2, 0, 3, 1, 4).reshape(N_AX, N_RAD, 4 * extent)
    return (all_maps, all_fluxes)
```

```python
import jax
import jax.numpy as jnp
from jax import lax
from jax.experimental import pallas as pl
from jax.experimental.pallas import tpu as pltpu
from jax.sharding import PartitionSpec as P

F32 = jnp.float32
VMEM_LIMIT = 56 * 1024 * 1024
NT = (((1,), (1,)), ((), ()))
NN = (((1,), (0,)), ((), ()))
TN = (((0,), (0,)), ((), ()))

ORDERS = ((0, 2, 3, 1), (0, 1, 2, 3), (2, 0, 3, 1), (0, 2, 1, 3))


def swapped(value, axis):
    count = lax.axis_size(axis)
    pairs = [(source, source ^ (count // 2)) for source in range(count)]
    return lax.ppermute(value, axis, pairs)


def halves():
    axial_bit = lax.axis_index("ax") // (lax.axis_size("ax") // 2)
    radial_bit = lax.axis_index("rad") // (lax.axis_size("rad") // 2)
    return axial_bit, radial_bit


def full_dot(a, b, dims):
    return lax.dot_general(
        a, b, dims, precision=lax.Precision.HIGHEST, preferred_element_type=F32
    )


def split(a):
    high = a.astype(jnp.bfloat16)
    low = (a - high.astype(F32)).astype(jnp.bfloat16)
    return high, low


def dot3(a, b, dims):
    a_high, a_low = split(a)
    b_high, b_low = split(b)
    total = lax.dot_general(a_high, b_low, dims, preferred_element_type=F32)
    total += lax.dot_general(a_low, b_high, dims, preferred_element_type=F32)
    return total + lax.dot_general(a_high, b_high, dims, preferred_element_type=F32)


def invert_factors(tiles):
    size = tiles[0].shape[0]
    count = size // 8
    lane = lax.broadcasted_iota(jnp.int32, (1, size), 1)
    sub = lax.broadcasted_iota(jnp.int32, (8, 1), 0)
    works = [[t[8 * i : 8 * i + 8, :] for i in range(count)] for t in tiles]
    for k in range(size):
        t0, s0 = k // 8, k % 8
        here = lane == k
        for work in works:
            row = work[t0][s0 : s0 + 1, :]
            inverse = 1.0 / work[t0][s0 : s0 + 1, k : k + 1]
            scaled = jnp.where(here, 1.0, row) * inverse
            for t in range(t0, count):
                if t == t0 and s0 == 7:
                    continue
                part = work[t]
                column = part[:, k : k + 1]
                fresh = jnp.where(here, 0.0, part) - column * scaled
                if t == t0:
                    fresh = jnp.where(sub > s0, fresh, part)
                work[t] = fresh
    results = []
    lanes = lax.broadcasted_iota(jnp.int32, (size, size), 1)
    rows = lax.broadcasted_iota(jnp.int32, (size, size), 0)
    for work in works:
        whole = jnp.concatenate(work, axis=0)
        pivots = jnp.sum(jnp.where(lanes == rows, whole, 0.0), axis=1, keepdims=True)
        unit = jnp.where(lanes < rows, whole, jnp.where(lanes == rows, 1.0, 0.0))
        results.append(unit * lax.rsqrt(pivots))
    return results


def factor_into(work, out, step):
    n = out.shape[0]
    work[:, n:] = (
        lax.broadcasted_iota(jnp.int32, (n, n), 0) == lax.broadcasted_iota(jnp.int32, (n, n), 1)
    ).astype(F32)

    @pl.loop(0, n // step)
    def _(b):
        start = pl.multiple_of(b * step, step)
        inverse = invert_factors([work[pl.ds(start, step), pl.ds(start, step)]])[0]
        panel = full_dot(inverse, work[pl.ds(start, step), :], NN)
        out[pl.ds(start, step), :] = panel[:, n:]
        lanes = lax.broadcasted_iota(jnp.int32, (step, n), 1)
        tail = jnp.where(lanes >= start + step, panel[:, :n], 0.0)
        work[...] -= full_dot(tail, panel, TN)


def call(kernel, shapes, scratch, flops, *args):
    moved = sum(a.size * 4 for a in args)
    return pl.pallas_call(
        kernel,
        out_shape=[jax.ShapeDtypeStruct(s, F32) for s in shapes],
        in_specs=[pl.BlockSpec(memory_space=pltpu.VMEM)] * len(args),
        out_specs=[pl.BlockSpec(memory_space=pltpu.VMEM)] * len(shapes),
        scratch_shapes=[pltpu.VMEM(s, F32) for s in scratch],
        compiler_params=pltpu.CompilerParams(vmem_limit_bytes=VMEM_LIMIT),
        cost_estimate=pl.CostEstimate(
            flops=flops, bytes_accessed=2 * moved, transcendentals=0
        ),
    )(*args)


def local_kernel(maps, fluxes, radial, rest, axial, outer, coupled, pairs, work, inverse, both):
    e = maps.shape[2] // 4
    axial_bit, radial_bit = halves()

    def seg(s):
        return slice(s * e, (s + 1) * e)

    schurs = [maps[0, j, seg(1), seg(1)] + maps[1, j, seg(0), seg(0)] for j in range(2)]
    factors = invert_factors(schurs)
    flux = [None, None]
    places = []
    for j in range(2):
        meeting = 3 if j == 0 else 2
        sides = [(0, meeting), (1, meeting), (0, 0), (1, 1), (0, 5 - meeting), (1, 5 - meeting)]
        places.append(sides)
        for p, (i, s) in enumerate(sides):
            coupled[seg(p), :] = maps[i, j, seg(s), seg(1 - i)]
        scaled = dot3(coupled[...], factors[j], NT)
        product = dot3(scaled, scaled, NT)
        pairs[j] = -product
        for p, (i, s) in enumerate(sides):
            for q, (k, t) in enumerate(sides):
                if i == k:
                    pairs[j, seg(p), seg(q)] += maps[i, j, seg(s), seg(t)]
        hint = fluxes[0, j, :, seg(1)] + fluxes[1, j, :, seg(0)]
        solved = full_dot(hint, factors[j], NT)
        own = jnp.concatenate([fluxes[i, j, :, seg(s)] for i, s in sides], axis=1)
        flux[j] = own - full_dot(solved, scaled, NT)
    n = 2 * e
    work[:, :n] = pairs[0, :n, :n] + pairs[1, :n, :n]
    factor_into(work, inverse, e)
    lower = dot3(pairs[0, n:, :n], inverse[...], NT)
    upper = dot3(pairs[1, n:, :n], inverse[...], NT)
    hint = flux[0][:, :n] + flux[1][:, :n]
    solved = full_dot(hint, inverse[...], NT)
    outs = [
        flux[0][:, n:] - full_dot(solved, lower, NT),
        flux[1][:, n:] - full_dot(solved, upper, NT),
    ]
    both[: 4 * e, : 4 * e] = pairs[0, n:, n:] - dot3(lower, lower, NT)
    both[4 * e :, 4 * e :] = pairs[1, n:, n:] - dot3(upper, upper, NT)
    cross = dot3(upper, lower, NT)
    both[4 * e :, : 4 * e] = -cross
    both[: 4 * e, 4 * e :] = -dot3(lower, upper, NT)
    radial_in = [(1 - radial_bit) * 4 + 2, (1 - radial_bit) * 4 + 3]
    radial_out = [radial_bit * 4 + 2, radial_bit * 4 + 3]
    axial_in = [1 - axial_bit, 5 - axial_bit]
    axial_out = [axial_bit, axial_bit + 4]

    def rows_of(s):
        return pl.ds(pl.multiple_of(s * e, e), e)

    def pieces(target, row_list, column_list, first):
        for p, r in enumerate(row_list):
            for q, c in enumerate(column_list):
                target[(first + p) * e : (first + p + 1) * e, seg(q)] = both[rows_of(r), rows_of(c)]

    pieces(radial, radial_in, radial_in, 0)
    pieces(rest, axial_in + axial_out + radial_out, radial_in, 0)
    pieces(axial, axial_in + axial_out + radial_out, axial_in, 0)
    final = axial_out + radial_out
    for q, order in enumerate(ORDERS):

        @pl.when(2 * axial_bit + radial_bit == q)
        def _():
            ordered = [final[o] for o in order]
            pieces(outer, ordered, ordered, 0)

    def chosen(flag, one, nought):
        return jnp.where(flag == 1, one, nought)

    zero, one = outs
    low = jnp.concatenate([zero[:, seg(0)], one[:, seg(0)]], axis=1)
    high = jnp.concatenate([zero[:, seg(1)], one[:, seg(1)]], axis=1)
    radial[2 * e : 2 * e + 1, :] = chosen(radial_bit, zero[:, 2 * e :], one[:, 2 * e :])
    radial[2 * e + 1 : 2 * e + 2, :] = chosen(axial_bit, low, high)
    radial[2 * e + 2 : 2 * e + 3, :] = chosen(axial_bit, high, low)
    radial[2 * e + 3 : 2 * e + 4, :] = chosen(radial_bit, one[:, 2 * e :], zero[:, 2 * e :])
    radial[2 * e + 4 :, :] = jnp.zeros((4, 2 * e), F32)


def factor_kernel(one, two, inverse, solved, work):
    n = inverse.shape[0]
    work[:, :n] = one[:n, :] + two[:n, :]
    factor_into(work, inverse, 128)
    hint = one[n : n + 1, :] + two[n : n + 1, :]
    solved[...] = full_dot(hint, inverse[...], NT)


def first_kernel(
    inverse, solved, radial, radial_far, rest, rest_far, axial, axial_far,
    schur, outer, scaled, remaining,
):
    n = inverse.shape[0]
    own = dot3(rest[...], inverse[...], NT)
    far = dot3(rest_far[...], inverse[...], NT)
    scaled[0] = own[n:, :]
    scaled[1] = far[n:, :]
    own_in, far_in = own[:n, :], far[:n, :]
    parts = ((axial[...], own), (-dot3(own, far_in, NT), own), (-dot3(far, own_in, NT), far))
    near = axial[...] - dot3(own, own_in, NT)
    opposite = axial_far[...] - dot3(far, far_in, NT)
    schur[:n, :n] = near[:n, :]
    schur[:n, n:] = parts[1][0][:n, :]
    schur[n : 2 * n, :n] = parts[2][0][:n, :]
    schur[n : 2 * n, n:] = opposite[:n, :]
    outer[: 2 * n, :n] = near[n:, :]
    outer[: 2 * n, n:] = parts[1][0][n:, :]
    outer[2 * n :, :n] = parts[2][0][n:, :]
    outer[2 * n :, n:] = opposite[n:, :]
    own_flux = full_dot(solved[...], own, NT)
    far_flux = full_dot(solved[...], far_in, NT)
    schur[2 * n : 2 * n + 1, :n] = radial[n + 1 : n + 2, :] - own_flux[:, :n]
    schur[2 * n : 2 * n + 1, n:] = radial_far[n + 1 : n + 2, :] - far_flux
    schur[2 * n + 1 :, :] = jnp.zeros((7, 2 * n), F32)
    remaining[:, :n] = radial[n + 2 : n + 3, :] - own_flux[:, n : 2 * n]
    remaining[:, n:] = radial[n + 3 : n + 4, :] - own_flux[:, 2 * n :]


def last_kernel(
    inverse, solved, outer, outer_far, scaled, remaining, own_map, merged, merged_flux, rows, mine
):
    n = inverse.shape[0]
    e = n // 4
    axial_bit, radial_bit = halves()
    quarter = 2 * axial_bit + radial_bit

    @pl.loop(0, 4)
    def _(slot):
        start = pl.multiple_of(lax.rem(slot, 2) * n, n)

        @pl.when(slot < 2)
        def _():
            rows[slot, :, :n] = dot3(outer[pl.ds(start, n), :], inverse[...], NT)
            rows[slot, :, n:] = scaled[slot]

        @pl.when(slot >= 2)
        def _():
            rows[slot, :, :n] = dot3(outer_far[pl.ds(start, n), :], inverse[...], NT)
            rows[slot, :, n:] = jnp.zeros((n, n // 2), F32)

    flux = remaining[...] - full_dot(solved[...], rows[0, :, :n], NT)
    for q, order in enumerate(ORDERS):

        @pl.when(quarter == q)
        def _():
            for p, o in enumerate(order):
                mine[p * e : (p + 1) * e, :] = rows[0, o * e : (o + 1) * e, :]
                merged_flux[:, p * e : (p + 1) * e] = flux[:, o * e : (o + 1) * e]

    for q, order in enumerate(ORDERS):
        slot = (axial_bit + q // 2) % 2 * 2 + (radial_bit + q % 2) % 2
        taken = jnp.concatenate([rows[slot, o * e : (o + 1) * e, :] for o in order], axis=0)
        product = dot3(mine[...], taken, NT)
        merged[:, q * n : (q + 1) * n] = jnp.where(quarter == q, own_map[...], 0.0) - product


def shards(leaf_maps, leaf_fluxes):
    e = leaf_maps.shape[2] // 4
    n = 2 * e
    radial, rest, axial, own_map = call(
        local_kernel,
        [(n + 8, n), (3 * n, n), (3 * n, n), (2 * n, 2 * n)],
        [(6 * e, e), (2, 6 * e, 6 * e), (n, 2 * n), (n, n), (8 * e, 8 * e)],
        10**9,
        leaf_maps,
        leaf_fluxes[:, :, None, :],
    )
    radial_far = swapped(radial, "rad")
    rest_far = swapped(rest, "rad")
    axial_far = swapped(axial, "rad")
    inverse, solved = call(
        factor_kernel, [(n, n), (1, n)], [(n, 2 * n)], 4 * 10**9, radial, radial_far
    )
    schur, outer, scaled, remaining = call(
        first_kernel,
        [(2 * n + 8, 2 * n), (4 * n, 2 * n), (2, 2 * n, n), (1, 2 * n)],
        [],
        10**9,
        inverse, solved, radial, radial_far, rest, rest_far, axial, axial_far,
    )
    schur_far = swapped(schur, "ax")
    outer_far = swapped(outer, "ax")
    inverse, solved = call(
        factor_kernel,
        [(2 * n, 2 * n), (1, 2 * n)],
        [(2 * n, 4 * n)],
        8 * 10**9,
        schur,
        schur_far,
    )
    merged, merged_flux = call(
        last_kernel,
        [(2 * n, 8 * n), (1, 2 * n)],
        [(4, 2 * n, 3 * n), (2 * n, 3 * n)],
        10**9,
        inverse, solved, outer, outer_far, scaled, remaining, own_map,
    )
    return merged[None, None], merged_flux[None]


def solution(mesh):
    in_specs = (P("ax", "rad", None, None), P("ax", "rad", None))
    out_specs = (P("ax", "rad", None, None), P("ax", "rad", None))
    return jax.shard_map(shards, mesh=mesh, in_specs=in_specs, out_specs=out_specs, check_vma=False)
```

```python
import jax
import jax.numpy as jnp
from jax import lax
from jax.experimental import pallas as pl
from jax.experimental.pallas import tpu as pltpu
from jax.sharding import PartitionSpec as P

F32 = jnp.float32
VMEM_LIMIT = 56 * 1024 * 1024
NT = (((1,), (1,)), ((), ()))
NN = (((1,), (0,)), ((), ()))
TN = (((0,), (0,)), ((), ()))

ORDERS = ((0, 2, 3, 1), (0, 1, 2, 3), (2, 0, 3, 1), (0, 2, 1, 3))


def swapped(value, axis):
    count = lax.axis_size(axis)
    pairs = [(source, source ^ (count // 2)) for source in range(count)]
    return lax.ppermute(value, axis, pairs)


def halves():
    axial_bit = lax.axis_index("ax") // (lax.axis_size("ax") // 2)
    radial_bit = lax.axis_index("rad") // (lax.axis_size("rad") // 2)
    return axial_bit, radial_bit


def full_dot(a, b, dims):
    return lax.dot_general(
        a, b, dims, precision=lax.Precision.HIGHEST, preferred_element_type=F32
    )


def split(a):
    high = a.astype(jnp.bfloat16)
    low = (a - high.astype(F32)).astype(jnp.bfloat16)
    return high, low


def dot3(a, b, dims):
    a_high, a_low = split(a)
    b_high, b_low = split(b)
    total = lax.dot_general(a_high, b_low, dims, preferred_element_type=F32)
    total += lax.dot_general(a_low, b_high, dims, preferred_element_type=F32)
    return total + lax.dot_general(a_high, b_high, dims, preferred_element_type=F32)


def invert_factors(tiles):
    size = tiles[0].shape[0]
    count = size // 8
    lane = lax.broadcasted_iota(jnp.int32, (8, size), 1)
    sub = lax.broadcasted_iota(jnp.int32, (8, size), 0)

    def spread(row):
        return jnp.broadcast_to(row, (8, size))

    works = [[t[8 * i : 8 * i + 8, :] for i in range(count)] for t in tiles]
    scales = [[None] * count for _ in tiles]
    for t0 in range(count):
        first = 8 * t0
        inside = (lane >= first) & (lane < first + 8)
        for work, scale in zip(works, scales):
            part = work[t0]
            columns = [spread(part[:, first + c : first + c + 1]) for c in range(8)]
            part = jnp.where(inside, (lane == sub + first).astype(F32), part)
            pivots = columns[0]
            rows, factors = [], []
            for s in range(8):
                if s:
                    pivots = jnp.where(sub >= s, columns[s], pivots)
                inverse = 1.0 / spread(columns[s][s : s + 1, :])
                rows.append(spread(part[s : s + 1, :]) * inverse)
                factors.append([spread(columns[c][s : s + 1, :]) * inverse for c in range(s + 1, 8)])
                lower = jnp.where(sub > s, columns[s], 0.0)
                part = part - lower * rows[s]
                for c in range(s + 1, 8):
                    columns[c] = columns[c] - lower * factors[s][c - s - 1]
            work[t0] = part
            scale[t0] = pivots
            for t in range(t0 + 1, count):
                part = work[t]
                columns = [spread(part[:, first + c : first + c + 1]) for c in range(8)]
                part = jnp.where(inside, 0.0, part)
                for s in range(8):
                    part = part - columns[s] * rows[s]
                    for c in range(s + 1, 8):
                        columns[c] = columns[c] - columns[s] * factors[s][c - s - 1]
                work[t] = part
    return [
        jnp.concatenate(
            [
                jnp.where(lane <= sub + 8 * i, work[i], 0.0) * lax.rsqrt(scale[i])
                for i in range(count)
            ],
            axis=0,
        )
        for work, scale in zip(works, scales)
    ]


def factor_into(work, out, step):
    n = out.shape[0]
    work[:, n:] = (
        lax.broadcasted_iota(jnp.int32, (n, n), 0) == lax.broadcasted_iota(jnp.int32, (n, n), 1)
    ).astype(F32)

    @pl.loop(0, n // step)
    def _(b):
        start = pl.multiple_of(b * step, step)
        inverse = invert_factors([work[pl.ds(start, step), pl.ds(start, step)]])[0]
        panel = dot3(inverse, work[pl.ds(start, step), :], NN)
        out[pl.ds(start, step), :] = panel[:, n:]
        lanes = lax.broadcasted_iota(jnp.int32, (step, n), 1)
        tail = jnp.where(lanes >= start + step, panel[:, :n], 0.0)
        work[...] -= dot3(tail, panel, TN)


def call(kernel, shapes, scratch, flops, *args):
    moved = sum(a.size * 4 for a in args)
    return pl.pallas_call(
        kernel,
        out_shape=[jax.ShapeDtypeStruct(s, F32) for s in shapes],
        in_specs=[pl.BlockSpec(memory_space=pltpu.VMEM)] * len(args),
        out_specs=[pl.BlockSpec(memory_space=pltpu.VMEM)] * len(shapes),
        scratch_shapes=[pltpu.VMEM(s, F32) for s in scratch],
        compiler_params=pltpu.CompilerParams(vmem_limit_bytes=VMEM_LIMIT),
        cost_estimate=pl.CostEstimate(
            flops=flops, bytes_accessed=2 * moved, transcendentals=0
        ),
    )(*args)


def local_kernel(maps, fluxes, radial, rest, axial, outer, coupled, pairs, work, inverse, both):
    e = maps.shape[2] // 4
    axial_bit, radial_bit = halves()

    def seg(s):
        return slice(s * e, (s + 1) * e)

    schurs = [maps[0, j, seg(1), seg(1)] + maps[1, j, seg(0), seg(0)] for j in range(2)]
    factors = invert_factors(schurs)
    flux = [None, None]
    places = []
    for j in range(2):
        meeting = 3 if j == 0 else 2
        sides = [(0, meeting), (1, meeting), (0, 0), (1, 1), (0, 5 - meeting), (1, 5 - meeting)]
        places.append(sides)
        for p, (i, s) in enumerate(sides):
            coupled[seg(p), :] = maps[i, j, seg(s), seg(1 - i)]
        scaled = dot3(coupled[...], factors[j], NT)
        product = dot3(scaled, scaled, NT)
        pairs[j] = -product
        for p, (i, s) in enumerate(sides):
            for q, (k, t) in enumerate(sides):
                if i == k:
                    pairs[j, seg(p), seg(q)] += maps[i, j, seg(s), seg(t)]
        hint = fluxes[0, j, :, seg(1)] + fluxes[1, j, :, seg(0)]
        solved = full_dot(hint, factors[j], NT)
        own = jnp.concatenate([fluxes[i, j, :, seg(s)] for i, s in sides], axis=1)
        flux[j] = own - full_dot(solved, scaled, NT)
    n = 2 * e
    work[:, :n] = pairs[0, :n, :n] + pairs[1, :n, :n]
    factor_into(work, inverse, e)
    lower = dot3(pairs[0, n:, :n], inverse[...], NT)
    upper = dot3(pairs[1, n:, :n], inverse[...], NT)
    hint = flux[0][:, :n] + flux[1][:, :n]
    solved = full_dot(hint, inverse[...], NT)
    outs = [
        flux[0][:, n:] - full_dot(solved, lower, NT),
        flux[1][:, n:] - full_dot(solved, upper, NT),
    ]
    both[: 4 * e, : 4 * e] = pairs[0, n:, n:] - dot3(lower, lower, NT)
    both[4 * e :, 4 * e :] = pairs[1, n:, n:] - dot3(upper, upper, NT)
    cross = dot3(upper, lower, NT)
    both[4 * e :, : 4 * e] = -cross
    both[: 4 * e, 4 * e :] = -dot3(lower, upper, NT)
    radial_in = [(1 - radial_bit) * 4 + 2, (1 - radial_bit) * 4 + 3]
    radial_out = [radial_bit * 4 + 2, radial_bit * 4 + 3]
    axial_in = [1 - axial_bit, 5 - axial_bit]
    axial_out = [axial_bit, axial_bit + 4]

    def rows_of(s):
        return pl.ds(pl.multiple_of(s * e, e), e)

    def pieces(target, row_list, column_list, first):
        for p, r in enumerate(row_list):
            for q, c in enumerate(column_list):
                target[(first + p) * e : (first + p + 1) * e, seg(q)] = both[rows_of(r), rows_of(c)]

    pieces(radial, radial_in, radial_in, 0)
    pieces(rest, axial_in + axial_out + radial_out, radial_in, 0)
    pieces(axial, axial_in + axial_out + radial_out, axial_in, 0)
    final = axial_out + radial_out
    for q, order in enumerate(ORDERS):

        @pl.when(2 * axial_bit + radial_bit == q)
        def _():
            ordered = [final[o] for o in order]
            pieces(outer, ordered, ordered, 0)

    def chosen(flag, one, nought):
        return jnp.where(flag == 1, one, nought)

    zero, one = outs
    low = jnp.concatenate([zero[:, seg(0)], one[:, seg(0)]], axis=1)
    high = jnp.concatenate([zero[:, seg(1)], one[:, seg(1)]], axis=1)
    radial[2 * e : 2 * e + 1, :] = chosen(radial_bit, zero[:, 2 * e :], one[:, 2 * e :])
    radial[2 * e + 1 : 2 * e + 2, :] = chosen(axial_bit, low, high)
    radial[2 * e + 2 : 2 * e + 3, :] = chosen(axial_bit, high, low)
    radial[2 * e + 3 : 2 * e + 4, :] = chosen(radial_bit, one[:, 2 * e :], zero[:, 2 * e :])
    radial[2 * e + 4 :, :] = jnp.zeros((4, 2 * e), F32)


def factor_kernel(one, two, inverse, solved, work):
    n = inverse.shape[0]
    work[:, :n] = one[:n, :] + two[:n, :]
    factor_into(work, inverse, 128)
    hint = one[n : n + 1, :] + two[n : n + 1, :]
    solved[...] = full_dot(hint, inverse[...], NT)


def first_kernel(
    inverse, solved, radial, radial_far, rest, rest_far, axial, axial_far,
    schur, outer, scaled, remaining,
):
    n = inverse.shape[0]
    own = dot3(rest[...], inverse[...], NT)
    far = dot3(rest_far[...], inverse[...], NT)
    scaled[0] = own[n:, :]
    scaled[1] = far[n:, :]
    own_in, far_in = own[:n, :], far[:n, :]
    parts = ((axial[...], own), (-dot3(own, far_in, NT), own), (-dot3(far, own_in, NT), far))
    near = axial[...] - dot3(own, own_in, NT)
    opposite = axial_far[...] - dot3(far, far_in, NT)
    schur[:n, :n] = near[:n, :]
    schur[:n, n:] = parts[1][0][:n, :]
    schur[n : 2 * n, :n] = parts[2][0][:n, :]
    schur[n : 2 * n, n:] = opposite[:n, :]
    outer[: 2 * n, :n] = near[n:, :]
    outer[: 2 * n, n:] = parts[1][0][n:, :]
    outer[2 * n :, :n] = parts[2][0][n:, :]
    outer[2 * n :, n:] = opposite[n:, :]
    own_flux = full_dot(solved[...], own, NT)
    far_flux = full_dot(solved[...], far_in, NT)
    schur[2 * n : 2 * n + 1, :n] = radial[n + 1 : n + 2, :] - own_flux[:, :n]
    schur[2 * n : 2 * n + 1, n:] = radial_far[n + 1 : n + 2, :] - far_flux
    schur[2 * n + 1 :, :] = jnp.zeros((7, 2 * n), F32)
    remaining[:, :n] = radial[n + 2 : n + 3, :] - own_flux[:, n : 2 * n]
    remaining[:, n:] = radial[n + 3 : n + 4, :] - own_flux[:, 2 * n :]


def last_kernel(
    inverse, solved, outer, outer_far, scaled, remaining, own_map, merged, merged_flux, rows, mine
):
    n = inverse.shape[0]
    e = n // 4
    axial_bit, radial_bit = halves()
    quarter = 2 * axial_bit + radial_bit

    @pl.loop(0, 4)
    def _(slot):
        start = pl.multiple_of(lax.rem(slot, 2) * n, n)

        @pl.when(slot < 2)
        def _():
            rows[slot, :, :n] = dot3(outer[pl.ds(start, n), :], inverse[...], NT)
            rows[slot, :, n:] = scaled[slot]

        @pl.when(slot >= 2)
        def _():
            rows[slot, :, :n] = dot3(outer_far[pl.ds(start, n), :], inverse[...], NT)
            rows[slot, :, n:] = jnp.zeros((n, n // 2), F32)

    flux = remaining[...] - full_dot(solved[...], rows[0, :, :n], NT)
    for q, order in enumerate(ORDERS):

        @pl.when(quarter == q)
        def _():
            for p, o in enumerate(order):
                mine[p * e : (p + 1) * e, :] = rows[0, o * e : (o + 1) * e, :]
                merged_flux[:, p * e : (p + 1) * e] = flux[:, o * e : (o + 1) * e]

    for q, order in enumerate(ORDERS):
        slot = (axial_bit + q // 2) % 2 * 2 + (radial_bit + q % 2) % 2
        taken = jnp.concatenate([rows[slot, o * e : (o + 1) * e, :] for o in order], axis=0)
        product = dot3(mine[...], taken, NT)
        merged[:, q * n : (q + 1) * n] = jnp.where(quarter == q, own_map[...], 0.0) - product


def shards(leaf_maps, leaf_fluxes):
    e = leaf_maps.shape[2] // 4
    n = 2 * e
    radial, rest, axial, own_map = call(
        local_kernel,
        [(n + 8, n), (3 * n, n), (3 * n, n), (2 * n, 2 * n)],
        [(6 * e, e), (2, 6 * e, 6 * e), (n, 2 * n), (n, n), (8 * e, 8 * e)],
        10**9,
        leaf_maps,
        leaf_fluxes[:, :, None, :],
    )
    radial_far = swapped(radial, "rad")
    radial_far, rest_late, axial_late = lax.optimization_barrier((radial_far, rest, axial))
    rest_far = swapped(rest_late, "rad")
    axial_far = swapped(axial_late, "rad")
    inverse, solved = call(
        factor_kernel, [(n, n), (1, n)], [(n, 2 * n)], 4 * 10**9, radial, radial_far
    )
    schur, outer, scaled, remaining = call(
        first_kernel,
        [(2 * n + 8, 2 * n), (4 * n, 2 * n), (2, 2 * n, n), (1, 2 * n)],
        [],
        10**9,
        inverse, solved, radial, radial_far, rest, rest_far, axial, axial_far,
    )
    schur_far = swapped(schur, "ax")
    schur_far, outer_late = lax.optimization_barrier((schur_far, outer))
    outer_far = swapped(outer_late, "ax")
    inverse, solved = call(
        factor_kernel,
        [(2 * n, 2 * n), (1, 2 * n)],
        [(2 * n, 4 * n)],
        8 * 10**9,
        schur,
        schur_far,
    )
    merged, merged_flux = call(
        last_kernel,
        [(2 * n, 8 * n), (1, 2 * n)],
        [(4, 2 * n, 3 * n), (2 * n, 3 * n)],
        10**9,
        inverse, solved, outer, outer_far, scaled, remaining, own_map,
    )
    return merged[None, None], merged_flux[None]


def solution(mesh):
    in_specs = (P("ax", "rad", None, None), P("ax", "rad", None))
    out_specs = (P("ax", "rad", None, None), P("ax", "rad", None))
    return jax.shard_map(shards, mesh=mesh, in_specs=in_specs, out_specs=out_specs, check_vma=False)
```

```python
import jax
import jax.numpy as jnp
from jax import lax
from jax.experimental import pallas as pl
from jax.experimental.pallas import tpu as pltpu
from jax.sharding import PartitionSpec as P

F32 = jnp.float32
VMEM_LIMIT = 56 * 1024 * 1024
NT = (((1,), (1,)), ((), ()))
NN = (((1,), (0,)), ((), ()))
TN = (((0,), (0,)), ((), ()))

ORDERS = ((0, 2, 3, 1), (0, 1, 2, 3), (2, 0, 3, 1), (0, 2, 1, 3))


def swapped(value, axis):
    count = lax.axis_size(axis)
    pairs = [(source, source ^ (count // 2)) for source in range(count)]
    return lax.ppermute(value, axis, pairs)


def halves():
    axial_bit = lax.axis_index("ax") // (lax.axis_size("ax") // 2)
    radial_bit = lax.axis_index("rad") // (lax.axis_size("rad") // 2)
    return axial_bit, radial_bit


def full_dot(a, b, dims):
    return lax.dot_general(
        a, b, dims, precision=lax.Precision.HIGHEST, preferred_element_type=F32
    )


def split(a):
    high = a.astype(jnp.bfloat16)
    low = (a - high.astype(F32)).astype(jnp.bfloat16)
    return high, low


def dot3(a, b, dims):
    a_high, a_low = split(a)
    b_high, b_low = split(b)
    total = lax.dot_general(a_high, b_low, dims, preferred_element_type=F32)
    total += lax.dot_general(a_low, b_high, dims, preferred_element_type=F32)
    return total + lax.dot_general(a_high, b_high, dims, preferred_element_type=F32)


def invert_factors(tiles):
    size = tiles[0].shape[0]
    count = size // 8
    lane = lax.broadcasted_iota(jnp.int32, (8, size), 1)
    sub = lax.broadcasted_iota(jnp.int32, (8, size), 0)

    def spread(row):
        return jnp.broadcast_to(row, (8, size))

    works = [[t[8 * i : 8 * i + 8, :] for i in range(count)] for t in tiles]
    scales = [[None] * count for _ in tiles]
    for t0 in range(count):
        first = 8 * t0
        inside = (lane >= first) & (lane < first + 8)
        for work, scale in zip(works, scales):
            part = work[t0]
            columns = [spread(part[:, first + c : first + c + 1]) for c in range(8)]
            part = jnp.where(inside, (lane == sub + first).astype(F32), part)
            pivots = columns[0]
            rows, factors = [], []
            for s in range(8):
                if s:
                    pivots = jnp.where(sub >= s, columns[s], pivots)
                inverse = 1.0 / spread(columns[s][s : s + 1, :])
                rows.append(spread(part[s : s + 1, :]) * inverse)
                factors.append([spread(columns[c][s : s + 1, :]) * inverse for c in range(s + 1, 8)])
                lower = jnp.where(sub > s, columns[s], 0.0)
                part = part - lower * rows[s]
                for c in range(s + 1, 8):
                    columns[c] = columns[c] - lower * factors[s][c - s - 1]
            work[t0] = part
            scale[t0] = pivots
            for t in range(t0 + 1, count):
                part = work[t]
                columns = [spread(part[:, first + c : first + c + 1]) for c in range(8)]
                part = jnp.where(inside, 0.0, part)
                for s in range(8):
                    part = part - columns[s] * rows[s]
                    for c in range(s + 1, 8):
                        columns[c] = columns[c] - columns[s] * factors[s][c - s - 1]
                work[t] = part
    return [
        jnp.concatenate(
            [
                jnp.where(lane <= sub + 8 * i, work[i], 0.0) * lax.rsqrt(scale[i])
                for i in range(count)
            ],
            axis=0,
        )
        for work, scale in zip(works, scales)
    ]


def factor_into(work, out, step):
    n = out.shape[0]
    work[:, n:] = (
        lax.broadcasted_iota(jnp.int32, (n, n), 0) == lax.broadcasted_iota(jnp.int32, (n, n), 1)
    ).astype(F32)

    @pl.loop(0, n // step)
    def _(b):
        start = pl.multiple_of(b * step, step)
        inverse = invert_factors([work[pl.ds(start, step), pl.ds(start, step)]])[0]
        panel = dot3(inverse, work[pl.ds(start, step), :], NN)
        out[pl.ds(start, step), :] = panel[:, n:]
        lanes = lax.broadcasted_iota(jnp.int32, (step, n), 1)
        tail = jnp.where(lanes >= start + step, panel[:, :n], 0.0)
        work[...] -= dot3(tail, panel, TN)


def call(kernel, shapes, scratch, flops, *args):
    moved = sum(a.size * 4 for a in args)
    return pl.pallas_call(
        kernel,
        out_shape=[jax.ShapeDtypeStruct(s, F32) for s in shapes],
        in_specs=[pl.BlockSpec(memory_space=pltpu.VMEM)] * len(args),
        out_specs=[pl.BlockSpec(memory_space=pltpu.VMEM)] * len(shapes),
        scratch_shapes=[pltpu.VMEM(s, F32) for s in scratch],
        compiler_params=pltpu.CompilerParams(vmem_limit_bytes=VMEM_LIMIT),
        cost_estimate=pl.CostEstimate(
            flops=flops, bytes_accessed=2 * moved, transcendentals=0
        ),
    )(*args)


def local_kernel(
    maps, fluxes, radial, rest, meet, side, outer, coupled, pairs, work, inverse, both
):
    e = maps.shape[2] // 4
    axial_bit, radial_bit = halves()

    def seg(s):
        return slice(s * e, (s + 1) * e)

    schurs = [maps[0, j, seg(1), seg(1)] + maps[1, j, seg(0), seg(0)] for j in range(2)]
    factors = invert_factors(schurs)
    flux = [None, None]
    places = []
    for j in range(2):
        meeting = 3 if j == 0 else 2
        sides = [(0, meeting), (1, meeting), (0, 0), (1, 1), (0, 5 - meeting), (1, 5 - meeting)]
        places.append(sides)
        for p, (i, s) in enumerate(sides):
            coupled[seg(p), :] = maps[i, j, seg(s), seg(1 - i)]
        scaled = dot3(coupled[...], factors[j], NT)
        product = dot3(scaled, scaled, NT)
        pairs[j] = -product
        for p, (i, s) in enumerate(sides):
            for q, (k, t) in enumerate(sides):
                if i == k:
                    pairs[j, seg(p), seg(q)] += maps[i, j, seg(s), seg(t)]
        hint = fluxes[0, j, :, seg(1)] + fluxes[1, j, :, seg(0)]
        solved = full_dot(hint, factors[j], NT)
        own = jnp.concatenate([fluxes[i, j, :, seg(s)] for i, s in sides], axis=1)
        flux[j] = own - full_dot(solved, scaled, NT)
    n = 2 * e
    work[:, :n] = pairs[0, :n, :n] + pairs[1, :n, :n]
    factor_into(work, inverse, e)
    lower = dot3(pairs[0, n:, :n], inverse[...], NT)
    upper = dot3(pairs[1, n:, :n], inverse[...], NT)
    hint = flux[0][:, :n] + flux[1][:, :n]
    solved = full_dot(hint, inverse[...], NT)
    outs = [
        flux[0][:, n:] - full_dot(solved, lower, NT),
        flux[1][:, n:] - full_dot(solved, upper, NT),
    ]
    both[: 4 * e, : 4 * e] = pairs[0, n:, n:] - dot3(lower, lower, NT)
    both[4 * e :, 4 * e :] = pairs[1, n:, n:] - dot3(upper, upper, NT)
    cross = dot3(upper, lower, NT)
    both[4 * e :, : 4 * e] = -cross
    both[: 4 * e, 4 * e :] = -dot3(lower, upper, NT)
    radial_in = [(1 - radial_bit) * 4 + 2, (1 - radial_bit) * 4 + 3]
    radial_out = [radial_bit * 4 + 2, radial_bit * 4 + 3]
    axial_in = [1 - axial_bit, 5 - axial_bit]
    axial_out = [axial_bit, axial_bit + 4]

    def rows_of(s):
        return pl.ds(pl.multiple_of(s * e, e), e)

    def pieces(target, row_list, column_list, first):
        for p, r in enumerate(row_list):
            for q, c in enumerate(column_list):
                target[(first + p) * e : (first + p + 1) * e, seg(q)] = both[rows_of(r), rows_of(c)]

    pieces(radial, radial_in, radial_in, 0)
    pieces(rest, axial_in + axial_out + radial_out, radial_in, 0)
    pieces(meet, axial_in, axial_in, 0)
    pieces(side, axial_out + radial_out, axial_in, 0)
    final = axial_out + radial_out
    for q, order in enumerate(ORDERS):

        @pl.when(2 * axial_bit + radial_bit == q)
        def _():
            ordered = [final[o] for o in order]
            pieces(outer, ordered, ordered, 0)

    def chosen(flag, one, nought):
        return jnp.where(flag == 1, one, nought)

    zero, one = outs
    low = jnp.concatenate([zero[:, seg(0)], one[:, seg(0)]], axis=1)
    high = jnp.concatenate([zero[:, seg(1)], one[:, seg(1)]], axis=1)
    radial[2 * e : 2 * e + 1, :] = chosen(radial_bit, zero[:, 2 * e :], one[:, 2 * e :])
    radial[2 * e + 1 : 2 * e + 2, :] = chosen(axial_bit, low, high)
    radial[2 * e + 2 : 2 * e + 3, :] = chosen(axial_bit, high, low)
    radial[2 * e + 3 : 2 * e + 4, :] = chosen(radial_bit, one[:, 2 * e :], zero[:, 2 * e :])
    radial[2 * e + 4 :, :] = jnp.zeros((4, 2 * e), F32)


def factor_kernel(one, two, inverse, solved, work):
    n = inverse.shape[0]
    work[:, :n] = one[:n, :] + two[:n, :]
    factor_into(work, inverse, 128)
    hint = one[n : n + 1, :] + two[n : n + 1, :]
    solved[...] = full_dot(hint, inverse[...], NT)


def first_kernel(
    inverse, solved, radial, radial_far, rest, rest_far, thin, scaled, remaining
):
    n = inverse.shape[0]
    own = dot3(rest[...], inverse[...], NT)
    far = dot3(rest_far[...], inverse[...], NT)
    thin[:n, :] = own[:n, :]
    thin[n : 2 * n, :] = far[:n, :]
    scaled[0] = own[n:, :]
    scaled[1] = far[n:, :]
    own_flux = full_dot(solved[...], own, NT)
    far_flux = full_dot(solved[...], far[:n, :], NT)
    thin[2 * n : 2 * n + 1, :] = radial[n + 1 : n + 2, :] - own_flux[:, :n]
    thin[2 * n + 1 : 2 * n + 2, :] = radial_far[n + 1 : n + 2, :] - far_flux
    thin[2 * n + 2 :, :] = jnp.zeros((6, n), F32)
    remaining[:, :n] = radial[n + 2 : n + 3, :] - own_flux[:, n : 2 * n]
    remaining[:, n:] = radial[n + 3 : n + 4, :] - own_flux[:, 2 * n :]


def second_factor_kernel(
    meet, meet_far, thin, thin_far, inverse, solved, bent, bent_far, work
):
    m = inverse.shape[0]
    n = m // 2
    own, far = thin[:m, :], thin_far[:m, :]
    work[:, :m] = -(dot3(own, own, NT) + dot3(far, far, NT))
    work[:n, :n] += meet[...]
    work[n:, n:m] += meet_far[...]
    factor_into(work, inverse, 128)
    hint = jnp.concatenate(
        [thin[m + i : m + i + 1, :] + thin_far[m + i : m + i + 1, :] for i in range(2)], axis=1
    )
    solved[...] = full_dot(hint, inverse[...], NT)
    bent[...] = dot3(inverse[...], own, NN)
    bent_far[...] = dot3(inverse[...], far, NN)


def rows_kernel(
    inverse, solved, bent, bent_far, side, side_rad, side_ax, scaled, scaled_far, remaining,
    rows, flux,
):
    n = bent.shape[1]
    low, high = inverse[:, :n], inverse[:, n:]
    rows[0] = dot3(side[...], low, NT) - dot3(scaled[0], bent[...], NT)
    rows[1] = dot3(side_rad[...], high, NT) - dot3(scaled[1], bent[...], NT)
    rows[2] = dot3(side_ax[...], low, NT) - dot3(scaled_far[0], bent_far[...], NT)
    flux[...] = remaining[...] - full_dot(solved[...], rows[0], NT)


def last_kernel(
    inverse, bent_far, side_diag, scaled, scaled_far, known, flux, own_map,
    merged, merged_flux, rows, mine,
):
    m = inverse.shape[0]
    n = m // 2
    e = n // 2
    axial_bit, radial_bit = halves()
    quarter = 2 * axial_bit + radial_bit
    for slot in range(3):
        rows[slot, :, :m] = known[slot]
    rows[3, :, :m] = dot3(side_diag[...], inverse[:, n:], NT) - dot3(
        scaled_far[1], bent_far[...], NT
    )
    for slot in range(4):
        rows[slot, :, m:] = scaled[slot] if slot < 2 else jnp.zeros((m, n), F32)
    for q, order in enumerate(ORDERS):

        @pl.when(quarter == q)
        def _():
            for p, o in enumerate(order):
                mine[p * e : (p + 1) * e, :] = rows[0, o * e : (o + 1) * e, :]
                merged_flux[:, p * e : (p + 1) * e] = flux[:, o * e : (o + 1) * e]

    for q, order in enumerate(ORDERS):
        slot = (axial_bit + q // 2) % 2 * 2 + (radial_bit + q % 2) % 2
        taken = jnp.concatenate([rows[slot, o * e : (o + 1) * e, :] for o in order], axis=0)
        product = dot3(mine[...], taken, NT)
        merged[:, q * m : (q + 1) * m] = jnp.where(quarter == q, own_map[...], 0.0) - product


def after(done, value):
    return lax.optimization_barrier((done, value))


def shards(leaf_maps, leaf_fluxes):
    e = leaf_maps.shape[2] // 4
    n = 2 * e
    m = 2 * n
    radial, rest, meet, side, own_map = call(
        local_kernel,
        [(n + 8, n), (3 * n, n), (n, n), (m, n), (m, m)],
        [(6 * e, e), (2, 6 * e, 6 * e), (n, m), (n, n), (8 * e, 8 * e)],
        10**9,
        leaf_maps,
        leaf_fluxes[:, :, None, :],
    )
    radial_far = swapped(radial, "rad")
    meet_ax = swapped(meet, "ax")
    side_ax = swapped(side, "ax")
    radial_far, rest_late = after(radial_far, rest)
    rest_far = swapped(rest_late, "rad")
    inverse, solved = call(
        factor_kernel, [(n, n), (1, n)], [(n, m)], 4 * 10**9, radial, radial_far
    )
    meet_sum = meet + meet_ax
    rest_far, meet_late = after(rest_far, meet_sum)
    meet_far = swapped(meet_late, "rad")
    thin, scaled, remaining = call(
        first_kernel,
        [(m + 8, n), (2, m, n), (1, m)],
        [],
        10**9,
        inverse, solved, radial, radial_far, rest, rest_far,
    )
    thin_far = swapped(thin, "ax")
    meet_far, side_late = after(meet_far, side)
    side_rad = swapped(side_late, "rad")
    thin_far, scaled_late = after(thin_far, scaled)
    scaled_far = swapped(scaled_late, "ax")
    inverse, solved, bent, bent_far = call(
        second_factor_kernel,
        [(m, m), (1, m), (m, n), (m, n)],
        [(m, 2 * m)],
        8 * 10**9,
        meet_sum, meet_far, thin, thin_far,
    )
    inverse, side_rad = after(inverse, side_rad)
    side_diag = swapped(side_rad, "ax")
    known, flux = call(
        rows_kernel,
        [(3, m, m), (1, m)],
        [],
        4 * 10**9,
        inverse, solved, bent, bent_far, side, side_rad, side_ax, scaled, scaled_far, remaining,
    )
    merged, merged_flux = call(
        last_kernel,
        [(m, 4 * m), (1, m)],
        [(4, m, 3 * n), (m, 3 * n)],
        10**9,
        inverse, bent_far, side_diag, scaled, scaled_far, known, flux, own_map,
    )
    return merged[None, None], merged_flux[None]


def solution(mesh):
    in_specs = (P("ax", "rad", None, None), P("ax", "rad", None))
    out_specs = (P("ax", "rad", None, None), P("ax", "rad", None))
    return jax.shard_map(shards, mesh=mesh, in_specs=in_specs, out_specs=out_specs, check_vma=False)
```

```python
import jax
import jax.numpy as jnp
from jax import lax
from jax.experimental import pallas as pl
from jax.experimental.pallas import tpu as pltpu
from jax.sharding import PartitionSpec as P

F32 = jnp.float32
VMEM_LIMIT = 56 * 1024 * 1024
NT = (((1,), (1,)), ((), ()))
NN = (((1,), (0,)), ((), ()))
TN = (((0,), (0,)), ((), ()))

ORDERS = ((0, 2, 3, 1), (0, 1, 2, 3), (2, 0, 3, 1), (0, 2, 1, 3))


def swapped(value, axis):
    count = lax.axis_size(axis)
    pairs = [(source, source ^ (count // 2)) for source in range(count)]
    return lax.ppermute(value, axis, pairs)


def halves():
    axial_bit = lax.axis_index("ax") // (lax.axis_size("ax") // 2)
    radial_bit = lax.axis_index("rad") // (lax.axis_size("rad") // 2)
    return axial_bit, radial_bit


def full_dot(a, b, dims):
    return lax.dot_general(
        a, b, dims, precision=lax.Precision.HIGHEST, preferred_element_type=F32
    )


def split(a):
    high = a.astype(jnp.bfloat16)
    low = (a - high.astype(F32)).astype(jnp.bfloat16)
    return high, low


def dot3(a, b, dims):
    a_high, a_low = split(a)
    b_high, b_low = split(b)
    total = lax.dot_general(a_high, b_low, dims, preferred_element_type=F32)
    total += lax.dot_general(a_low, b_high, dims, preferred_element_type=F32)
    return total + lax.dot_general(a_high, b_high, dims, preferred_element_type=F32)


def invert_factors(tiles):
    size = tiles[0].shape[0]
    count = size // 8
    lane = lax.broadcasted_iota(jnp.int32, (8, size), 1)
    sub = lax.broadcasted_iota(jnp.int32, (8, size), 0)

    def spread(row):
        return jnp.broadcast_to(row, (8, size))

    works = [[t[8 * i : 8 * i + 8, :] for i in range(count)] for t in tiles]
    scales = [[None] * count for _ in tiles]
    for t0 in range(count):
        first = 8 * t0
        inside = (lane >= first) & (lane < first + 8)
        for work, scale in zip(works, scales):
            part = work[t0]
            columns = [spread(part[:, first + c : first + c + 1]) for c in range(8)]
            part = jnp.where(inside, (lane == sub + first).astype(F32), part)
            pivots = columns[0]
            rows, factors = [], []
            for s in range(8):
                if s:
                    pivots = jnp.where(sub >= s, columns[s], pivots)
                inverse = 1.0 / spread(columns[s][s : s + 1, :])
                rows.append(spread(part[s : s + 1, :]) * inverse)
                factors.append([spread(columns[c][s : s + 1, :]) * inverse for c in range(s + 1, 8)])
                lower = jnp.where(sub > s, columns[s], 0.0)
                part = part - lower * rows[s]
                for c in range(s + 1, 8):
                    columns[c] = columns[c] - lower * factors[s][c - s - 1]
            work[t0] = part
            scale[t0] = pivots
            for t in range(t0 + 1, count):
                part = work[t]
                columns = [spread(part[:, first + c : first + c + 1]) for c in range(8)]
                part = jnp.where(inside, 0.0, part)
                for s in range(8):
                    part = part - columns[s] * rows[s]
                    for c in range(s + 1, 8):
                        columns[c] = columns[c] - columns[s] * factors[s][c - s - 1]
                work[t] = part
    return [
        jnp.concatenate(
            [
                jnp.where(lane <= sub + 8 * i, work[i], 0.0) * lax.rsqrt(scale[i])
                for i in range(count)
            ],
            axis=0,
        )
        for work, scale in zip(works, scales)
    ]


def factor_into(work, out, step):
    n = out.shape[0]
    work[:, n:] = (
        lax.broadcasted_iota(jnp.int32, (n, n), 0) == lax.broadcasted_iota(jnp.int32, (n, n), 1)
    ).astype(F32)

    @pl.loop(0, n // step)
    def _(b):
        start = pl.multiple_of(b * step, step)
        inverse = invert_factors([work[pl.ds(start, step), pl.ds(start, step)]])[0]
        panel = dot3(inverse, work[pl.ds(start, step), :], NN)
        out[pl.ds(start, step), :] = panel[:, n:]
        lanes = lax.broadcasted_iota(jnp.int32, (step, n), 1)
        tail = jnp.where(lanes >= start + step, panel[:, :n], 0.0)
        work[...] -= dot3(tail, panel, TN)


def call(kernel, shapes, scratch, flops, *args):
    moved = sum(a.size * 4 for a in args)
    return pl.pallas_call(
        kernel,
        out_shape=[jax.ShapeDtypeStruct(s, F32) for s in shapes],
        in_specs=[pl.BlockSpec(memory_space=pltpu.VMEM)] * len(args),
        out_specs=[pl.BlockSpec(memory_space=pltpu.VMEM)] * len(shapes),
        scratch_shapes=[pltpu.VMEM(s, F32) for s in scratch],
        compiler_params=pltpu.CompilerParams(vmem_limit_bytes=VMEM_LIMIT),
        cost_estimate=pl.CostEstimate(
            flops=flops, bytes_accessed=2 * moved, transcendentals=0
        ),
    )(*args)


def local_kernel(
    maps, fluxes, radial, rest, meet, side, outer, coupled, pairs, work, inverse, both
):
    e = maps.shape[2] // 4
    axial_bit, radial_bit = halves()

    def seg(s):
        return slice(s * e, (s + 1) * e)

    schurs = [maps[0, j, seg(1), seg(1)] + maps[1, j, seg(0), seg(0)] for j in range(2)]
    factors = invert_factors(schurs)
    flux = [None, None]
    places = []
    for j in range(2):
        meeting = 3 if j == 0 else 2
        sides = [(0, meeting), (1, meeting), (0, 0), (1, 1), (0, 5 - meeting), (1, 5 - meeting)]
        places.append(sides)
        for p, (i, s) in enumerate(sides):
            coupled[seg(p), :] = maps[i, j, seg(s), seg(1 - i)]
        scaled = dot3(coupled[...], factors[j], NT)
        product = dot3(scaled, scaled, NT)
        pairs[j] = -product
        for p, (i, s) in enumerate(sides):
            for q, (k, t) in enumerate(sides):
                if i == k:
                    pairs[j, seg(p), seg(q)] += maps[i, j, seg(s), seg(t)]
        hint = fluxes[0, j, :, seg(1)] + fluxes[1, j, :, seg(0)]
        solved = full_dot(hint, factors[j], NT)
        own = jnp.concatenate([fluxes[i, j, :, seg(s)] for i, s in sides], axis=1)
        flux[j] = own - full_dot(solved, scaled, NT)
    n = 2 * e
    work[:, :n] = pairs[0, :n, :n] + pairs[1, :n, :n]
    factor_into(work, inverse, e)
    lower = dot3(pairs[0, n:, :n], inverse[...], NT)
    upper = dot3(pairs[1, n:, :n], inverse[...], NT)
    hint = flux[0][:, :n] + flux[1][:, :n]
    solved = full_dot(hint, inverse[...], NT)
    outs = [
        flux[0][:, n:] - full_dot(solved, lower, NT),
        flux[1][:, n:] - full_dot(solved, upper, NT),
    ]
    both[: 4 * e, : 4 * e] = pairs[0, n:, n:] - dot3(lower, lower, NT)
    both[4 * e :, 4 * e :] = pairs[1, n:, n:] - dot3(upper, upper, NT)
    cross = dot3(upper, lower, NT)
    both[4 * e :, : 4 * e] = -cross
    both[: 4 * e, 4 * e :] = -dot3(lower, upper, NT)
    radial_in = [(1 - radial_bit) * 4 + 2, (1 - radial_bit) * 4 + 3]
    radial_out = [radial_bit * 4 + 2, radial_bit * 4 + 3]
    axial_in = [1 - axial_bit, 5 - axial_bit]
    axial_out = [axial_bit, axial_bit + 4]

    def rows_of(s):
        return pl.ds(pl.multiple_of(s * e, e), e)

    def pieces(target, row_list, column_list, first):
        for p, r in enumerate(row_list):
            for q, c in enumerate(column_list):
                target[(first + p) * e : (first + p + 1) * e, seg(q)] = both[rows_of(r), rows_of(c)]

    pieces(radial, radial_in, radial_in, 0)
    pieces(rest, axial_in + axial_out + radial_out, radial_in, 0)
    pieces(meet, axial_in, axial_in, 0)
    pieces(side, axial_out + radial_out, axial_in, 0)
    final = axial_out + radial_out
    for q, order in enumerate(ORDERS):

        @pl.when(2 * axial_bit + radial_bit == q)
        def _():
            ordered = [final[o] for o in order]
            pieces(outer, ordered, ordered, 0)

    def chosen(flag, one, nought):
        return jnp.where(flag == 1, one, nought)

    zero, one = outs
    low = jnp.concatenate([zero[:, seg(0)], one[:, seg(0)]], axis=1)
    high = jnp.concatenate([zero[:, seg(1)], one[:, seg(1)]], axis=1)
    radial[2 * e : 2 * e + 1, :] = chosen(radial_bit, zero[:, 2 * e :], one[:, 2 * e :])
    radial[2 * e + 1 : 2 * e + 2, :] = chosen(axial_bit, low, high)
    radial[2 * e + 2 : 2 * e + 3, :] = chosen(axial_bit, high, low)
    radial[2 * e + 3 : 2 * e + 4, :] = chosen(radial_bit, one[:, 2 * e :], zero[:, 2 * e :])
    radial[2 * e + 4 :, :] = jnp.zeros((4, 2 * e), F32)


def factor_kernel(one, two, inverse, solved, work):
    n = inverse.shape[0]
    work[:, :n] = one[:n, :] + two[:n, :]
    factor_into(work, inverse, 128)
    hint = one[n : n + 1, :] + two[n : n + 1, :]
    solved[...] = full_dot(hint, inverse[...], NT)


def first_kernel(
    inverse, solved, radial, radial_far, rest, rest_far, thin, scaled, remaining
):
    n = inverse.shape[0]
    own = dot3(rest[...], inverse[...], NT)
    far = dot3(rest_far[...], inverse[...], NT)
    thin[:n, :] = own[:n, :]
    thin[n : 2 * n, :] = far[:n, :]
    scaled[0] = own[n:, :]
    scaled[1] = far[n:, :]
    own_flux = full_dot(solved[...], own, NT)
    far_flux = full_dot(solved[...], far[:n, :], NT)
    thin[2 * n : 2 * n + 1, :] = radial[n + 1 : n + 2, :] - own_flux[:, :n]
    thin[2 * n + 1 : 2 * n + 2, :] = radial_far[n + 1 : n + 2, :] - far_flux
    thin[2 * n + 2 :, :] = jnp.zeros((6, n), F32)
    remaining[:, :n] = radial[n + 2 : n + 3, :] - own_flux[:, n : 2 * n]
    remaining[:, n:] = radial[n + 3 : n + 4, :] - own_flux[:, 2 * n :]


def second_factor_kernel(
    meet, meet_far, thin, thin_far, inverse, solved, bent, bent_far, work
):
    m = inverse.shape[0]
    n = m // 2
    own, far = thin[:m, :], thin_far[:m, :]
    work[:, :m] = -(dot3(own, own, NT) + dot3(far, far, NT))
    work[:n, :n] += meet[...]
    work[n:, n:m] += meet_far[...]
    factor_into(work, inverse, 128)
    hint = jnp.concatenate(
        [thin[m + i : m + i + 1, :] + thin_far[m + i : m + i + 1, :] for i in range(2)], axis=1
    )
    solved[...] = full_dot(hint, inverse[...], NT)
    bent[...] = dot3(inverse[...], own, NN)
    bent_far[...] = dot3(inverse[...], far, NN)


def rows_kernel(
    inverse, solved, bent, bent_far, side, side_rad, side_ax, scaled, scaled_far, remaining,
    rows, flux,
):
    n = bent.shape[1]
    low, high = inverse[:, :n], inverse[:, n:]
    rows[0] = dot3(side[...], low, NT) - dot3(scaled[0], bent[...], NT)
    rows[1] = dot3(side_rad[...], high, NT) - dot3(scaled[1], bent[...], NT)
    rows[2] = dot3(side_ax[...], low, NT) - dot3(scaled_far[0], bent_far[...], NT)
    flux[...] = remaining[...] - full_dot(solved[...], rows[0], NT)


def last_kernel(
    inverse, bent_far, side_diag, scaled, scaled_far, known, flux, own_map,
    merged, merged_flux, rows, mine,
):
    m = inverse.shape[0]
    n = m // 2
    e = n // 2
    axial_bit, radial_bit = halves()
    quarter = 2 * axial_bit + radial_bit
    for slot in range(3):
        rows[slot, :, :m] = known[slot]
    rows[3, :, :m] = dot3(side_diag[...], inverse[:, n:], NT) - dot3(
        scaled_far[1], bent_far[...], NT
    )
    for slot in range(4):
        rows[slot, :, m:] = scaled[slot] if slot < 2 else jnp.zeros((m, n), F32)
    for q, order in enumerate(ORDERS):

        @pl.when(quarter == q)
        def _():
            for p, o in enumerate(order):
                mine[p * e : (p + 1) * e, :] = rows[0, o * e : (o + 1) * e, :]
                merged_flux[:, p * e : (p + 1) * e] = flux[:, o * e : (o + 1) * e]

    for q, order in enumerate(ORDERS):
        slot = (axial_bit + q // 2) % 2 * 2 + (radial_bit + q % 2) % 2
        taken = jnp.concatenate([rows[slot, o * e : (o + 1) * e, :] for o in order], axis=0)
        product = dot3(mine[...], taken, NT)
        merged[:, q * m : (q + 1) * m] = jnp.where(quarter == q, own_map[...], 0.0) - product


def after(done, value):
    return lax.optimization_barrier((done, value))


def shards(leaf_maps, leaf_fluxes):
    e = leaf_maps.shape[2] // 4
    n = 2 * e
    m = 2 * n
    radial, rest, meet, side, own_map = call(
        local_kernel,
        [(n + 8, n), (3 * n, n), (n, n), (m, n), (m, m)],
        [(6 * e, e), (2, 6 * e, 6 * e), (n, m), (n, n), (8 * e, 8 * e)],
        10**9,
        leaf_maps,
        leaf_fluxes[:, :, None, :],
    )
    radial_far = swapped(radial, "rad")
    meet_ax = swapped(meet, "ax")
    side_ax = swapped(side, "ax")
    rest_far = swapped(rest, "rad")
    inverse, solved = call(
        factor_kernel, [(n, n), (1, n)], [(n, m)], 4 * 10**9, radial, radial_far
    )
    inverse, meet_ax, side_ax = lax.optimization_barrier((inverse, meet_ax, side_ax))
    meet_sum = meet + meet_ax
    rest_far, meet_late = after(rest_far, meet_sum)
    meet_far = swapped(meet_late, "rad")
    thin, scaled, remaining = call(
        first_kernel,
        [(m + 8, n), (2, m, n), (1, m)],
        [],
        10**9,
        inverse, solved, radial, radial_far, rest, rest_far,
    )
    thin_far = swapped(thin, "ax")
    meet_far, side_late = after(meet_far, side)
    side_rad = swapped(side_late, "rad")
    thin_far, scaled_late = after(thin_far, scaled)
    scaled_far = swapped(scaled_late, "ax")
    inverse, solved, bent, bent_far = call(
        second_factor_kernel,
        [(m, m), (1, m), (m, n), (m, n)],
        [(m, 2 * m)],
        8 * 10**9,
        meet_sum, meet_far, thin, thin_far,
    )
    inverse, side_rad = after(inverse, side_rad)
    side_diag = swapped(side_rad, "ax")
    known, flux = call(
        rows_kernel,
        [(3, m, m), (1, m)],
        [],
        4 * 10**9,
        inverse, solved, bent, bent_far, side, side_rad, side_ax, scaled, scaled_far, remaining,
    )
    merged, merged_flux = call(
        last_kernel,
        [(m, 4 * m), (1, m)],
        [(4, m, 3 * n), (m, 3 * n)],
        10**9,
        inverse, bent_far, side_diag, scaled, scaled_far, known, flux, own_map,
    )
    return merged[None, None], merged_flux[None]


def solution(mesh):
    in_specs = (P("ax", "rad", None, None), P("ax", "rad", None))
    out_specs = (P("ax", "rad", None, None), P("ax", "rad", None))
    return jax.shard_map(shards, mesh=mesh, in_specs=in_specs, out_specs=out_specs, check_vma=False)
```
